32 devices in a mesh: ctx: 8 (over z, y), head: 4 (over x, core).
Axes of the slice: x: 2, y: 2, z: 4, core: 2. Of those that a mesh axis runs over, the one named last changes fastest.
Arguments:
- tokens: bfloat16 [3072, 4096], P('ctx', 'head'), may hold values from -6 to 6
- doc_ids: int32 [3072], replicated, may hold values from 0 to 3, never falling along the last dimension, each value on 1 to 2304 neighbouring positions
- norm_gain: float32 [4096], replicated, may hold values from 0.25 to 1.75
- w_query: bfloat16 [4096, 4096], P(None, 'head'), may hold values from -4 to 4
- w_key: bfloat16 [4096, 1024], P(None, 'head'), may hold values from -0.09375 to 0.09375
- w_value: bfloat16 [4096, 1024], P(None, 'head'), may hold values from -0.09375 to 0.09375
- w_out: bfloat16 [4096, 4096], P('head'), may hold values from -0.09375 to 0.09375
Outputs:
- layer_out: bfloat16 [3072, 4096], P('ctx', 'head')
The draws below stay inside these ranges and needn't reach their ends.
Inputs may be any that keep to these rules, and one draw needn't show every extreme that they name: `doc_ids`: never falling along the sequence; 4 documents, one of exactly 2304 tokens.
All inputs are finite; a program needn't handle non-finite values.
Results may differ from the reference program's by a relative error of at most 0.012.
The reference program's roundings to bfloat16 on the way count: a program that leaves them out, or rounds other values in their place, can miss the bound.
Values may be sent and summed in bfloat16 or wider, within the bound.
No kernel may reach another device: no remote copies, remote signals or barrier semaphores. Data moves between devices by JAX's collectives and lax.ppermute only.
A program may use at most 128 MiB of HBM per device.

```python
import math
import jax
import jax.numpy as jnp
import numpy as np
from jax import lax

D = 4096
HQ = 32
KVH = 8
HD = 128
TOK_DEV = 384
DOCS = 4
TOKENS = 3072
N_CTX = 8


def draw_w_query(key, part):
    sample = jax.random.truncated_normal(key, -6.0, 6.0, (D, HQ * HD), jnp.float32) * D ** (-0.5)
    sample = jnp.clip(sample, -4.0, 4.0)
    return sample.astype(jnp.bfloat16)


def shard_levels(own_key, dims, split, least, largest):
    loudness = 1.0
    for axis_at, blocks in split:
        heights = jax.random.uniform(jax.random.fold_in(jax.random.fold_in(own_key, 6), axis_at), (blocks,), jnp.float32, least / len(split), largest / len(split))
        loudness = loudness * jnp.repeat(jnp.exp(heights), dims[axis_at] // blocks).reshape((-1,) + (1,) * (len(dims) - 1 - axis_at))
    return loudness


def split_up(amount, total, limit, lean):
    portions = [(1 << 20) // math.isqrt(grade ** lean) + 1 for grade in range(2, amount + 1)]
    surplus, holding = total - limit - (amount - 1), [1] * (amount - 1)
    while surplus > 0:
        candidates = [i for i in range(amount - 1) if holding[i] < limit]
        pool, left = sum([portions[i] for i in candidates]), surplus
        for i in candidates:
            more = min(limit - holding[i], max(1, left * portions[i] // pool), surplus)
            holding[i] = holding[i] + more
            surplus = surplus - more
    return np.array([limit] + holding)


def ragged_sizes(key, number_of, total, reach, lean):
    if number_of == 2:
        one = jax.random.randint(key, (), max(1, total - reach), min(reach, total - 1) + 1)
        return jnp.stack([one, total - one])
    sizes = jnp.asarray(split_up(number_of, total, reach, lean), jnp.int32)
    twos = (number_of - 1) // 2
    donor, sink = sizes[1:1 + 2 * twos:2], sizes[2:2 + 2 * twos:2]
    margin = jnp.minimum(donor - 1, reach - sink)
    moved = jax.random.randint(jax.random.fold_in(key, 1), (twos,), 0, 1 << 20) % (margin + 1)
    sizes = sizes.at[1:1 + 2 * twos:2].set(donor - moved).at[2:2 + 2 * twos:2].set(sink + moved)
    return sizes[jax.random.permutation(jax.random.fold_in(key, 2), number_of)]


def gaussian(stream_key, extent, scale, reach, pieces=(), kind=jnp.bfloat16):
    level = shard_levels(stream_key, extent, pieces, -0.22, 0.18) if pieces else 1.0
    array = jax.random.normal(stream_key, extent, jnp.float32) * scale * level
    return jnp.minimum(jnp.maximum(array, -reach), reach).astype(kind)


def setup_inputs(seed: int = 0) -> dict:
    arg_keys = jax.random.split(jax.random.key(seed), 8)
    tokens = gaussian(arg_keys[0], (TOKENS, D), 1.0, 6.0, ((0, 8), (1, 4)))
    doc_ids = jnp.searchsorted(jnp.cumsum(ragged_sizes(arg_keys[1], DOCS, TOKENS, 3 * TOKENS // 4, 2)), jnp.arange(TOKENS), side="right").astype(jnp.int32)
    norm_gain = jnp.clip(1.0 + 0.15 * jax.random.normal(arg_keys[2], (D,), jnp.float32), 0.25, 1.75)
    w_query = draw_w_query(jax.random.fold_in(arg_keys[7], 71), 0)
    w_key = gaussian(arg_keys[4], (D, KVH * HD), D ** -0.5, 0.09375, ((1, 4),))
    w_value = gaussian(arg_keys[5], (D, KVH * HD), D ** -0.5, 0.09375, ((1, 4),))
    w_out = gaussian(arg_keys[6], (HQ * HD, D), (HQ * HD) ** -0.5, 0.09375, ((0, 4),))
    return dict(tokens=tokens, doc_ids=doc_ids, norm_gain=norm_gain, w_query=w_query, w_key=w_key, w_value=w_value, w_out=w_out)


THETA = 500000.0

def rotate(values, positions):
    head_width = values.shape[-1]
    midpoint = head_width // 2
    exponents = jnp.arange(midpoint, dtype=jnp.float32) * (2.0 / head_width)
    inverse = jnp.power(jnp.float32(THETA), -exponents)
    angles = positions.astype(jnp.float32)[:, None] * inverse[None, :]
    cosine = jnp.cos(angles)[:, None, :]
    sine_wave = jnp.sin(angles)[:, None, :]
    lower_half = values[..., :midpoint]
    upper_half = values[..., midpoint:]
    return jnp.concatenate([lower_half * cosine - upper_half * sine_wave, upper_half * cosine + lower_half * sine_wave], axis=-1)

def reference(tokens, doc_ids, norm_gain, w_query, w_key, w_value, w_out):
    floats = tokens.astype(jnp.float32)
    spread = lax.optimization_barrier(jnp.mean(floats * floats, axis=-1, keepdims=True))
    normed = (floats * lax.rsqrt(spread + 1e-05) * norm_gain[None, :]).astype(jnp.bfloat16)
    positions = jnp.arange(TOKENS, dtype=jnp.int32)
    queries = jnp.dot(normed, w_query, preferred_element_type=jnp.float32).reshape(TOKENS, HQ, HD)
    queries = rotate(queries, positions).astype(jnp.bfloat16)
    keys_all = jnp.dot(normed, w_key, preferred_element_type=jnp.float32).reshape(TOKENS, KVH, HD)
    keys_all = rotate(keys_all, positions).astype(jnp.bfloat16)
    values_all = jnp.dot(normed, w_value, preferred_element_type=jnp.float32).astype(jnp.bfloat16).reshape(TOKENS, KVH, HD)
    starts = jnp.searchsorted(doc_ids, doc_ids, side='left').astype(jnp.int32)
    query_heads = jnp.transpose(queries, (1, 0, 2))
    key_heads = jnp.transpose(keys_all, (1, 0, 2))
    value_heads = jnp.transpose(values_all, (1, 0, 2))
    group_size = HQ // KVH
    score_scale = HD ** (-0.5)

    def one_head(head_index):
        query_rows = query_heads[head_index]
        key_rows = key_heads[head_index // group_size]
        value_rows = value_heads[head_index // group_size]

        def one_block(block_index):
            row_start = block_index * TOK_DEV
            block_queries = lax.dynamic_slice_in_dim(query_rows, row_start, TOK_DEV, 0)
            block_positions = lax.dynamic_slice_in_dim(positions, row_start, TOK_DEV, 0)
            block_starts = lax.dynamic_slice_in_dim(starts, row_start, TOK_DEV, 0)
            scores = jnp.dot(block_queries, key_rows.T, preferred_element_type=jnp.float32) * score_scale
            allowed = (positions[None, :] <= block_positions[:, None]) & (positions[None, :] >= block_starts[:, None])
            scores = jnp.where(allowed, scores, -jnp.inf)
            highest = lax.optimization_barrier(jnp.max(scores, axis=-1, keepdims=True))
            weights = jnp.where(allowed, jnp.exp(scores - highest), 0.0)
            denominator = lax.optimization_barrier(jnp.sum(weights, axis=-1, keepdims=True))
            combined = jnp.dot(weights.astype(jnp.bfloat16), value_rows, preferred_element_type=jnp.float32)
            return combined / denominator
        return lax.map(one_block, jnp.arange(N_CTX, dtype=jnp.int32)).reshape(TOKENS, HD)
    heads_out = lax.map(one_head, jnp.arange(HQ, dtype=jnp.int32))
    attended = jnp.transpose(heads_out, (1, 0, 2)).reshape(TOKENS, HQ * HD).astype(jnp.bfloat16)
    return (floats + jnp.dot(attended, w_out, preferred_element_type=jnp.float32)).astype(jnp.bfloat16)
```

```python
import functools
import math

import jax
import jax.numpy as jnp
from jax import lax
from jax.experimental import pallas as pl
from jax.experimental.pallas import tpu as pltpu
from jax.sharding import PartitionSpec as P

HD = 128
THETA = 500000.0
SENTINEL = -1e30
CHUNKS = 3
F32 = jnp.float32
BF16 = jnp.bfloat16


def rope_tables(positions):
    midpoint = HD // 2
    exponents = jnp.arange(midpoint, dtype=F32) * (2.0 / HD)
    inverse = jnp.power(F32(THETA), -exponents)
    angles = positions.astype(F32)[:, None] * inverse[None, :]
    cosine, sine = jnp.cos(angles), jnp.sin(angles)
    return (
        jnp.concatenate([cosine, cosine], axis=-1),
        jnp.concatenate([-sine, sine], axis=-1),
    )


def rope(v, cosine, sine):
    half = HD // 2
    turned = jnp.concatenate([v[:, half:], v[:, :half]], axis=-1)
    return v * cosine + turned * sine


def kv_kernel(h_ref, t, tm, x, xm, gain, wk, wv, cosine, sine, normed, kv):
    h = h_ref[0]
    width = t.shape[1]
    total = 0.0
    for block in (t, tm, x, xm):
        f = block[...].astype(F32)
        total = total + jnp.sum(f * f, axis=-1, keepdims=True)
    scale = lax.rsqrt(total / (4 * width) + 1e-05)
    for step, block in enumerate((t, tm, x, xm)):
        at = pl.ds(pl.multiple_of((h ^ step) * width, width), width)
        f = block[...].astype(F32)
        normed[:, at] = (f * scale * gain[:, at]).astype(BF16)
    n = normed[...]
    kdim = wk.shape[1]
    k = jnp.dot(n, wk[...], preferred_element_type=F32)
    for j in range(kdim // HD):
        kv[:, j * HD : (j + 1) * HD] = rope(
            k[:, j * HD : (j + 1) * HD], cosine[...], sine[...]
        ).astype(BF16)
    kv[:, kdim:] = jnp.dot(n, wv[...], preferred_element_type=F32).astype(BF16)


def project_kv(h, r, rows, t, tm, x, xm, gain, wk, wv, cosine, sine):
    width = t.shape[1]
    kvdim = wk.shape[1] + wv.shape[1]

    def part(a):
        return pl.BlockSpec((rows, a.shape[1]), lambda i: (r, 0))

    def whole(a):
        return pl.BlockSpec(a.shape, lambda i: (0, 0))

    return pl.pallas_call(
        kv_kernel,
        grid=(1,),
        in_specs=[
            pl.BlockSpec(memory_space=pltpu.SMEM),
            part(t),
            part(tm),
            whole(x),
            whole(xm),
            whole(gain),
            whole(wk),
            whole(wv),
            part(cosine),
            part(sine),
        ],
        out_specs=[
            pl.BlockSpec((rows, 4 * width), lambda i: (0, 0)),
            pl.BlockSpec((rows, kvdim), lambda i: (0, 0)),
        ],
        out_shape=[
            jax.ShapeDtypeStruct((rows, 4 * width), BF16),
            jax.ShapeDtypeStruct((rows, kvdim), BF16),
        ],
        compiler_params=pltpu.CompilerParams(vmem_limit_bytes=40 << 20),
        cost_estimate=pl.CostEstimate(
            flops=2 * rows * 4 * width * kvdim, bytes_accessed=10 << 20, transcendentals=0
        ),
        name="project_kv",
    )(h, t, tm, x, xm, gain, wk, wv, cosine, sine)


def q_kernel(*refs):
    chunks = refs[:CHUNKS]
    wq, cosine, sine, q = refs[CHUNKS:]
    n = jnp.concatenate([c[...] for c in chunks], axis=0)
    y = jnp.dot(n, wq[...], preferred_element_type=F32)
    for j in range(wq.shape[1] // HD):
        at = slice(j * HD, (j + 1) * HD)
        q[:, at] = rope(y[:, at], cosine[...], sine[...]).astype(BF16)


def project_q(normed, wq, cosine, sine):
    rows = sum(c.shape[0] for c in normed)
    depth, cols = wq.shape
    block = 256

    def whole(a):
        return pl.BlockSpec(a.shape, lambda i: (0, 0))

    return pl.pallas_call(
        q_kernel,
        grid=(cols // block,),
        in_specs=[whole(c) for c in normed]
        + [pl.BlockSpec((depth, block), lambda i: (0, i)), whole(cosine), whole(sine)],
        out_specs=pl.BlockSpec((rows, block), lambda i: (0, i)),
        out_shape=jax.ShapeDtypeStruct((rows, cols), BF16),
        compiler_params=pltpu.CompilerParams(vmem_limit_bytes=40 << 20),
        cost_estimate=pl.CostEstimate(
            flops=2 * rows * depth * cols, bytes_accessed=12 << 20, transcendentals=0
        ),
        name="project_q",
    )(*normed, wq, cosine, sine)


def attend_kernel(slots, r, info, q, starts, *refs):
    pieces = refs[: slots * CHUNKS]
    out, kvbuf, qs, m, l, acc, sems = refs[slots * CHUNKS :]
    ctx, low, high = info[0], info[1], info[2]
    rows = q.shape[0]
    shard_rows = rows * CHUNKS
    kvh = kvbuf.shape[2] // (2 * HD)
    group = q.shape[1] // (kvh * HD)
    row_base = ctx * shard_rows + r * rows
    c2 = HD**-0.5 * math.log2(math.e)

    def shard_of(slot):
        odd = slot % 2
        return jnp.where(odd == 1, ctx ^ 1, ctx) - (slot - odd)

    def needed(shard):
        return (shard >= 0) & (shard <= ctx) & ((shard + 1) * shard_rows > low)

    for slot in range(slots):

        @pl.when(needed(shard_of(slot)))
        def _():
            for j in range(CHUNKS):
                pltpu.make_async_copy(
                    pieces[slot * CHUNKS + j],
                    kvbuf.at[slot, pl.ds(j * rows, rows)],
                    sems.at[slot, j],
                ).start()

    for g in range(kvh):
        for j in range(group):
            a = (g * group + j) * HD
            qs[g, j * rows : (j + 1) * rows, :] = q[:, a : a + HD]
    m[...] = jnp.full(m.shape, SENTINEL, F32)
    l[...] = jnp.zeros(l.shape, F32)
    acc[...] = jnp.zeros(acc.shape, F32)

    def step(slot, shard, masked):
        if masked:
            key_at = shard * shard_rows + lax.broadcasted_iota(
                jnp.int32, (rows, shard_rows), 1
            )
            row_at = row_base + lax.broadcasted_iota(jnp.int32, (rows, shard_rows), 0)
            allowed = (key_at <= row_at) & (key_at >= starts[...])
            bias = jnp.where(allowed, 0.0, SENTINEL)
        for g in range(kvh):
            k = kvbuf[slot, :, g * HD : (g + 1) * HD]
            v = kvbuf[slot, :, (kvh + g) * HD : (kvh + g + 1) * HD]
            s = lax.dot_general(
                qs[g], k, (((1,), (1,)), ((), ())), preferred_element_type=F32
            )
            if masked:
                s = jnp.where(
                    jnp.concatenate([bias] * group, axis=0) < 0.0, SENTINEL, s
                )
            old = m[g]
            new = jnp.maximum(old, jnp.max(s, axis=-1, keepdims=True))
            m[g] = new
            w = jnp.exp2((s - new[:, :1]) * c2)
            factor = jnp.exp2((old - new) * c2)
            part = w[:, :HD]
            for b in range(1, shard_rows // HD):
                part = part + w[:, b * HD : (b + 1) * HD]
            l[g] = l[g] * factor + part
            acc[g] = acc[g] * factor + jnp.dot(
                w.astype(BF16), v, preferred_element_type=F32
            )

    def visit(slot, carry):
        shard = shard_of(slot)

        @pl.when(needed(shard))
        def _():
            for j in range(CHUNKS):
                pltpu.make_async_copy(
                    pieces[0], kvbuf.at[slot, pl.ds(j * rows, rows)], sems.at[slot, j]
                ).wait()
            full = (shard < ctx) & (shard * shard_rows >= high)

            @pl.when(full)
            def _():
                step(slot, shard, False)

            @pl.when(jnp.logical_not(full))
            def _():
                step(slot, shard, True)

        return carry

    lax.fori_loop(0, slots, visit, 0)
    for g in range(kvh):
        total = jnp.sum(l[g], axis=-1, keepdims=True)
        done = (acc[g] / total).astype(BF16)
        for j in range(group):
            a = (g * group + j) * HD
            out[:, a : a + HD] = done[j * rows : (j + 1) * rows]


def attend(r, info, q, starts, pieces, kvh):
    rows, kvdim = pieces[0].shape
    slots = len(pieces) // CHUNKS
    cols = q.shape[1]
    group = cols // HD // kvh
    return pl.pallas_call(
        functools.partial(attend_kernel, slots, r),
        grid=(1,),
        in_specs=[
            pl.BlockSpec(memory_space=pltpu.SMEM),
            pl.BlockSpec((rows, cols), lambda i: (r, 0)),
            pl.BlockSpec((rows, 1), lambda i: (r, 0)),
        ]
        + [pl.BlockSpec(memory_space=pl.ANY)] * len(pieces),
        out_specs=pl.BlockSpec((rows, cols), lambda i: (0, 0)),
        out_shape=jax.ShapeDtypeStruct((rows, cols), BF16),
        scratch_shapes=[
            pltpu.VMEM((slots, rows * CHUNKS, kvdim), BF16),
            pltpu.VMEM((kvh, group * rows, HD), BF16),
            pltpu.VMEM((kvh, group * rows, HD), F32),
            pltpu.VMEM((kvh, group * rows, HD), F32),
            pltpu.VMEM((kvh, group * rows, HD), F32),
            pltpu.SemaphoreType.DMA((slots, CHUNKS)),
        ],
        compiler_params=pltpu.CompilerParams(vmem_limit_bytes=40 << 20),
        cost_estimate=pl.CostEstimate(
            flops=4 * rows * CHUNKS * rows * slots * cols,
            bytes_accessed=4 << 20,
            transcendentals=rows * CHUNKS * rows * slots * cols // HD,
        ),
        name="attend",
    )(info, q, starts, *pieces)


def out_kernel(info, a, am, w, wm, out):
    y = jnp.dot(a[...], w[...], preferred_element_type=F32)
    y = y + jnp.dot(am[...], wm[...], preferred_element_type=F32)
    out[...] = y.astype(out.dtype)


def project_out(info, a, am, w, wm, dtype):
    rows, depth = a.shape
    cols = wm.shape[1] // 2
    block = 512
    per = cols // block
    return pl.pallas_call(
        out_kernel,
        grid_spec=pltpu.PrefetchScalarGridSpec(
            num_scalar_prefetch=1,
            grid=(per,),
            in_specs=[
                pl.BlockSpec((rows, depth), lambda i, s: (0, 0)),
                pl.BlockSpec((rows, depth), lambda i, s: (0, 0)),
                pl.BlockSpec((depth, block), lambda i, s: (0, s[0] * per + i)),
                pl.BlockSpec((depth, block), lambda i, s: (0, s[1] * per + i)),
            ],
            out_specs=pl.BlockSpec((rows, block), lambda i, s: (0, i)),
        ),
        out_shape=jax.ShapeDtypeStruct((rows, cols), dtype),
        compiler_params=pltpu.CompilerParams(vmem_limit_bytes=40 << 20),
        cost_estimate=pl.CostEstimate(
            flops=4 * rows * depth * cols, bytes_accessed=5 << 20, transcendentals=0
        ),
        name="project_out",
    )(info, a, am, w, wm)


def on_device(n_ctx, n_head, tokens, doc_ids, norm_gain, w_query, w_key, w_value, w_out):
    rows, width = tokens.shape
    part = rows // CHUNKS
    ctx = lax.axis_index("ctx")
    head = lax.axis_index("head")
    kvh = w_key.shape[1] // HD
    longest = 3 * (rows * n_ctx) // 4

    def across(v, flip):
        return lax.ppermute(v, "head", [(i, i ^ flip) for i in range(n_head)])

    chunk = lambda v, r: lax.slice_in_dim(v, r * part, (r + 1) * part, axis=0)
    x = [across(chunk(tokens, r), 2) for r in range(CHUNKS)]
    tm = across(tokens, 1)
    xm = [across(v, 1) for v in x]

    core = head % 2
    theirs = lax.dynamic_index_in_dim(
        w_out.reshape(w_out.shape[0], 2, 2, width), 1 - core, axis=2, keepdims=False
    ).reshape(w_out.shape[0], 2 * width)
    wm = across(theirs, 1)

    positions = ctx * rows + jnp.arange(rows, dtype=jnp.int32)
    cosine, sine = rope_tables(positions)
    own_docs = lax.dynamic_slice_in_dim(doc_ids, ctx * rows, rows, 0)
    starts = jnp.sum(
        (doc_ids[None, :] < own_docs[:, None]).astype(jnp.int32), axis=1, keepdims=True
    )
    gain = norm_gain[None, :]
    heads = head.reshape(1).astype(jnp.int32)

    normed, kv = [], []
    for r in range(CHUNKS):
        n, y = project_kv(
            heads, r, part, tokens, tm, x[r], xm[r], gain, w_key, w_value, cosine, sine
        )
        normed.append(n)
        kv.append(y)
    q = project_q(normed, w_query, cosine, sine)

    def wanted(c, s):
        return 0 <= s <= c and (s + 1) * rows - 1 >= c * rows - (longest - 1)

    column, pieces = kv, []
    for k in range(n_ctx // 2):
        if k:
            pairs = [(c - 2, c) for c in range(2 * k, n_ctx)]
            pairs = [
                (a, c)
                for a, c in pairs
                if any(wanted(d, c - 2 * k) for d in range(c, n_ctx))
            ]
            column = [lax.ppermute(v, "ctx", pairs) for v in column]
        pairs = [(c ^ 1, c) for c in range(n_ctx) if wanted(c, (c ^ 1) - 2 * k)]
        pieces += column
        pieces += [lax.ppermute(v, "ctx", pairs) for v in column]

    outs = []
    for r in range(CHUNKS):
        info = jnp.stack([ctx, starts[r * part, 0], starts[(r + 1) * part - 1, 0]]).astype(
            jnp.int32
        )
        a = attend(r, info, q, starts, pieces, kvh)
        am = across(a, 1)
        away = jnp.stack([head ^ 2, (head // 2) ^ 1]).astype(jnp.int32)
        here = jnp.stack([head, head // 2]).astype(jnp.int32)
        sent = across(project_out(away, a, am, w_out, wm, BF16), 2)
        mine = project_out(here, a, am, w_out, wm, F32)
        outs.append(
            (sent.astype(F32) + mine + chunk(tokens, r).astype(F32)).astype(BF16)
        )
    return jnp.concatenate(outs, axis=0)


def solution(mesh):
    in_specs = (
        P("ctx", "head"),
        P(),
        P(),
        P(None, "head"),
        P(None, "head"),
        P(None, "head"),
        P("head", None),
    )
    body = functools.partial(on_device, mesh.shape["ctx"], mesh.shape["head"])
    return jax.shard_map(
        body, mesh=mesh, in_specs=in_specs, out_specs=P("ctx", "head"), check_vma=False
    )
```

```python
import functools
import math

import jax
import jax.numpy as jnp
from jax import lax
from jax.experimental import pallas as pl
from jax.experimental.pallas import tpu as pltpu
from jax.sharding import PartitionSpec as P

HD = 128
THETA = 500000.0
SENTINEL = -1e30
CHUNKS = 2
OUT_CHUNKS = 4
SCALE = HD**-0.5 * math.log2(math.e)
F32 = jnp.float32
BF16 = jnp.bfloat16
VMEM_LIMIT = 40 << 20
CTX, LOW, HIGH, HEAD = range(4)


def in_vmem(v):
    return pltpu.with_memory_space_constraint(v, pltpu.VMEM)


def in_hbm(v):
    return pltpu.with_memory_space_constraint(v, pltpu.HBM)


def whole(a):
    return pl.BlockSpec(a.shape, lambda *i: (0,) * a.ndim)


def rope_tables(positions):
    midpoint = HD // 2
    exponents = jnp.arange(midpoint, dtype=F32) * (2.0 / HD)
    inverse = jnp.power(F32(THETA), -exponents)
    angles = positions.astype(F32)[:, None] * inverse[None, :]
    cosine, sine = jnp.cos(angles), jnp.sin(angles)
    return (
        jnp.concatenate([cosine, cosine], axis=-1),
        jnp.concatenate([-sine, sine], axis=-1),
    )


def rope(v, cosine, sine):
    half = HD // 2
    turned = jnp.concatenate([v[:, half:], v[:, :half]], axis=-1)
    return v * cosine + turned * sine


def kv_kernel(info, t, tm, x, xm, gain, wk, wv, cosine, sine, normed, kv):
    head = info[HEAD]
    width = t.shape[1]
    total = 0.0
    for block in (t, tm, x, xm):
        f = block[...].astype(F32)
        total = total + jnp.sum(f * f, axis=-1, keepdims=True)
    scale = lax.rsqrt(total / (4 * width) + 1e-05)
    for step, block in enumerate((t, tm, x, xm)):
        at = pl.ds(pl.multiple_of((head ^ step) * width, width), width)
        f = block[...].astype(F32)
        normed[:, at] = (f * scale * gain[:, at]).astype(BF16)
    n = normed[...]
    kdim = wk.shape[1]
    k = jnp.dot(n, wk[...], preferred_element_type=F32)
    for j in range(kdim // HD):
        at = slice(j * HD, (j + 1) * HD)
        kv[:, at] = rope(k[:, at], cosine[...], sine[...]).astype(BF16)
    kv[:, kdim:] = jnp.dot(n, wv[...], preferred_element_type=F32).astype(BF16)


def project_kv(info, r, rows, t, tm, x, xm, gain, wk, wv, cosine, sine):
    width = t.shape[1]
    kvdim = wk.shape[1] + wv.shape[1]

    def part(a):
        return pl.BlockSpec((rows, a.shape[1]), lambda i: (r, 0))

    resident = pl.BlockSpec(memory_space=pltpu.VMEM)
    return pl.pallas_call(
        kv_kernel,
        grid=(1,),
        in_specs=[
            pl.BlockSpec(memory_space=pltpu.SMEM),
            part(t),
            part(tm),
            whole(x),
            whole(xm),
            whole(gain),
            resident,
            resident,
            part(cosine),
            part(sine),
        ],
        out_specs=[
            pl.BlockSpec((rows, 4 * width), lambda i: (0, 0)),
            pl.BlockSpec((rows, kvdim), lambda i: (0, 0)),
        ],
        out_shape=[
            jax.ShapeDtypeStruct((rows, 4 * width), BF16),
            jax.ShapeDtypeStruct((rows, kvdim), BF16),
        ],
        compiler_params=pltpu.CompilerParams(vmem_limit_bytes=VMEM_LIMIT),
        cost_estimate=pl.CostEstimate(
            flops=2 * rows * 4 * width * kvdim, bytes_accessed=10 << 20, transcendentals=0
        ),
        name="project_kv",
    )(info, t, tm, x, xm, gain, wk, wv, cosine, sine)


def q_kernel(*refs):
    chunks = refs[:CHUNKS]
    wq, cosine, sine, q = refs[CHUNKS:]
    n = jnp.concatenate([c[...] for c in chunks], axis=0)
    rows = n.shape[0]
    y = jnp.dot(n, wq[...], preferred_element_type=F32)
    for j in range(wq.shape[1] // HD):
        v = rope(y[:, j * HD : (j + 1) * HD], cosine[...], sine[...])
        q[j * rows : (j + 1) * rows, :] = (v * SCALE).astype(BF16)


def project_q(normed, wq, cosine, sine):
    rows = sum(c.shape[0] for c in normed)
    depth, cols = wq.shape
    block = 2 * HD
    return pl.pallas_call(
        q_kernel,
        grid=(cols // block,),
        in_specs=[whole(c) for c in normed]
        + [pl.BlockSpec((depth, block), lambda i: (0, i)), whole(cosine), whole(sine)],
        out_specs=pl.BlockSpec((2 * rows, HD), lambda i: (i, 0)),
        out_shape=jax.ShapeDtypeStruct((cols // HD * rows, HD), BF16),
        compiler_params=pltpu.CompilerParams(vmem_limit_bytes=VMEM_LIMIT),
        cost_estimate=pl.CostEstimate(
            flops=2 * rows * depth * cols, bytes_accessed=12 << 20, transcendentals=0
        ),
        name="project_q",
    )(*normed, in_hbm(wq), cosine, sine)


def attend_kernel(steps, first, last, info, q, starts, *refs):
    slots = len(steps)
    pieces = refs[: slots * CHUNKS]
    refs = refs[slots * CHUNKS :]
    before, refs = ((), refs) if first else (refs[:3], refs[3:])
    after, refs = (refs[:1], refs[1:]) if last else (refs[:3], refs[3:])
    kvbuf, m, l, acc, sems = refs
    ctx, low, high = info[CTX], info[LOW], info[HIGH]
    rows = starts.shape[0]
    part = rows // CHUNKS
    kvh, stacked = m.shape[:2]
    group = stacked // rows

    def shard_of(slot):
        odd = slot % 2
        return jnp.where(odd == 1, ctx ^ 1, ctx) - 2 * (steps[0][0] + slot // 2)

    def needed(shard):
        return (shard >= 0) & (shard <= ctx) & ((shard + 1) * rows > low)

    for slot in range(slots):

        @pl.when(needed(shard_of(slot)))
        def _():
            for j in range(CHUNKS):
                pltpu.make_async_copy(
                    pieces[slot * CHUNKS + j],
                    kvbuf.at[slot, pl.ds(j * part, part)],
                    sems.at[slot, j],
                ).start()

    if first:
        m[...] = jnp.full(m.shape, SENTINEL, F32)
        l[...] = jnp.zeros(l.shape, F32)
        acc[...] = jnp.zeros(acc.shape, F32)
    else:
        for new, old in zip((m, l, acc), before):
            new[...] = old[...]

    def step(slot, shard, masked):
        if masked:
            key_at = shard * rows + lax.broadcasted_iota(jnp.int32, (rows, rows), 1)
            row_at = ctx * rows + lax.broadcasted_iota(jnp.int32, (rows, rows), 0)
            allowed = (key_at <= row_at) & (key_at >= starts[...])
            allowed = jnp.concatenate([allowed] * group, axis=0)
        for g in range(kvh):
            k = kvbuf[slot, :, g * HD : (g + 1) * HD]
            v = kvbuf[slot, :, (kvh + g) * HD : (kvh + g + 1) * HD]
            s = lax.dot_general(
                q[g * stacked : (g + 1) * stacked, :],
                k,
                (((1,), (1,)), ((), ())),
                preferred_element_type=F32,
            )
            if masked:
                s = jnp.where(allowed, s, SENTINEL)
            tiles = [s[:, b * HD : (b + 1) * HD] for b in range(rows // HD)]
            old = m[g]
            top = functools.reduce(jnp.maximum, tiles)
            new = jnp.maximum(
                old, jnp.broadcast_to(jnp.max(top, axis=-1, keepdims=True), old.shape)
            )
            m[g] = new
            w = [jnp.exp2(t - new) for t in tiles]
            factor = jnp.exp2(old - new)
            l[g] = l[g] * factor + functools.reduce(jnp.add, w)
            w = jnp.concatenate([t.astype(BF16) for t in w], axis=1)
            acc[g] = acc[g] * factor + jnp.dot(w, v, preferred_element_type=F32)

    def visit(slot, carry):
        shard = shard_of(slot)

        @pl.when(needed(shard))
        def _():
            for j in range(CHUNKS):
                pltpu.make_async_copy(
                    pieces[0], kvbuf.at[slot, pl.ds(j * part, part)], sems.at[slot, j]
                ).wait()
            full = (shard < ctx) & (shard * rows >= high)

            @pl.when(full)
            def _():
                step(slot, shard, False)

            @pl.when(jnp.logical_not(full))
            def _():
                step(slot, shard, True)

        return carry

    lax.fori_loop(0, slots, visit, 0)
    if last:
        (out,) = after
        for g in range(kvh):
            total = jnp.sum(l[g], axis=-1, keepdims=True)
            done = (acc[g] / total).astype(BF16)
            for j in range(group):
                a = (g * group + j) * HD
                out[:, a : a + HD] = done[j * rows : (j + 1) * rows]
    else:
        for new, old in zip(after, (m, l, acc)):
            new[...] = old[...]


def attend(steps, pieces, info, q, starts, state, last, kvh):
    rows = starts.shape[0]
    kvdim = pieces[0].shape[1]
    heads = q.shape[0] // rows
    stacked = q.shape[0] // kvh
    slots = len(steps)
    carried = jax.ShapeDtypeStruct((kvh, stacked, HD), F32)
    resident = pl.BlockSpec(memory_space=pltpu.VMEM)
    if last:
        out_shape = [jax.ShapeDtypeStruct((rows, heads * HD), BF16)]
        out_specs = [pl.BlockSpec((rows, heads * HD), lambda i: (0, 0))]
    else:
        out_shape = [pltpu.VMEM(carried.shape, F32)] * 3
        out_specs = [resident] * 3
    state = [in_vmem(v) for v in state] if state else []
    return pl.pallas_call(
        functools.partial(attend_kernel, steps, not state, last),
        grid=(1,),
        in_specs=[pl.BlockSpec(memory_space=pltpu.SMEM), whole(q), whole(starts)]
        + [pl.BlockSpec(memory_space=pl.ANY)] * len(pieces)
        + [resident] * len(state),
        out_specs=out_specs,
        out_shape=out_shape,
        scratch_shapes=[
            pltpu.VMEM((slots, rows, kvdim), BF16),
            pltpu.VMEM(carried.shape, F32),
            pltpu.VMEM(carried.shape, F32),
            pltpu.VMEM(carried.shape, F32),
            pltpu.SemaphoreType.DMA((slots, CHUNKS)),
        ],
        compiler_params=pltpu.CompilerParams(vmem_limit_bytes=VMEM_LIMIT),
        cost_estimate=pl.CostEstimate(
            flops=4 * rows * rows * slots * heads * HD,
            bytes_accessed=2 << 20,
            transcendentals=rows * rows * slots * heads,
        ),
        name="attend",
    )(info, q, starts, *pieces, *state)


def out_kernel(info, a, am, w, wm, out):
    y = jnp.dot(a[...], w[...], preferred_element_type=F32)
    y = y + jnp.dot(am[...], wm[...], preferred_element_type=F32)
    out[...] = y.astype(out.dtype)


def project_out(info, flip, at, steps, a, am, w, wm, dtype):
    rows, depth = a.shape
    cols = wm[0].shape[1]
    block = cols // OUT_CHUNKS
    side = flip // 2

    def mates(i, s):
        return (0, at + i)

    return pl.pallas_call(
        out_kernel,
        grid_spec=pltpu.PrefetchScalarGridSpec(
            num_scalar_prefetch=1,
            grid=(steps,),
            in_specs=[
                pl.BlockSpec((rows, depth), lambda i, s: (0, 0)),
                pl.BlockSpec((rows, depth), lambda i, s: (0, 0)),
                pl.BlockSpec(
                    (depth, block), lambda i, s: (0, (s[HEAD] ^ flip) * OUT_CHUNKS + at + i)
                ),
                pl.BlockSpec((depth, block), mates),
            ],
            out_specs=pl.BlockSpec((rows, block), lambda i, s: (0, i)),
        ),
        out_shape=jax.ShapeDtypeStruct((rows, steps * block), dtype),
        compiler_params=pltpu.CompilerParams(vmem_limit_bytes=VMEM_LIMIT),
        cost_estimate=pl.CostEstimate(
            flops=4 * rows * depth * block * steps, bytes_accessed=5 << 20, transcendentals=0
        ),
        name="project_out",
    )(info, a, am, in_hbm(w), in_hbm(wm[side]))


def add_kernel(count, at, *refs):
    received, (mine, tokens), out = refs[:count], refs[count : count + 2], refs[-1]
    block = received[0].shape[1]
    for i, piece in enumerate(received):
        cols = slice(i * block, (i + 1) * block)
        total = piece[...].astype(F32) + mine[:, cols] + tokens[:, cols].astype(F32)
        out[:, cols] = total.astype(BF16)


def add_up(received, at, mine, tokens, out):
    rows, block = received[0].shape
    count = len(received)
    cols = block * count
    place = pl.BlockSpec((rows, cols), lambda i: (0, at // count))
    return pl.pallas_call(
        functools.partial(add_kernel, count, at),
        grid=(1,),
        in_specs=[whole(v) for v in received]
        + [place, place]
        + ([] if out is None else [pl.BlockSpec(memory_space=pl.ANY)]),
        out_specs=place,
        out_shape=jax.ShapeDtypeStruct(tokens.shape, BF16),
        input_output_aliases={} if out is None else {count + 2: 0},
        compiler_params=pltpu.CompilerParams(vmem_limit_bytes=VMEM_LIMIT),
        name="add_up",
    )(*received, mine, tokens, *([] if out is None else [out]))


def on_device(n_ctx, n_head, tokens, doc_ids, norm_gain, w_query, w_key, w_value, w_out):
    rows, width = tokens.shape
    part = rows // CHUNKS
    ctx = lax.axis_index("ctx")
    head = lax.axis_index("head")
    kvh = w_key.shape[1] // HD

    def across(v, flip):
        return lax.ppermute(v, "head", [(i, i ^ flip) for i in range(n_head)])

    def neighbour(v):
        return lax.ppermute(v, "ctx", [(i, i ^ 1) for i in range(n_ctx)])

    def upward(v):
        return lax.ppermute(v, "ctx", [(i, (i + 2) % n_ctx) for i in range(n_ctx)])

    x = [
        across(lax.slice_in_dim(tokens, r * part, (r + 1) * part, axis=0), 2)
        for r in range(CHUNKS)
    ]
    tm = across(tokens, 1)
    xm = [across(v, 1) for v in x]

    positions = ctx * rows + jnp.arange(rows, dtype=jnp.int32)
    cosine, sine = rope_tables(positions)
    own_docs = lax.dynamic_slice_in_dim(doc_ids, ctx * rows, rows, 0)
    starts = jnp.sum(
        (doc_ids[None, :] < own_docs[:, None]).astype(jnp.int32), axis=1, keepdims=True
    )
    info = jnp.stack([ctx, starts[0, 0], starts[rows - 1, 0], head]).astype(jnp.int32)
    gain = norm_gain[None, :]

    wk, wv = in_vmem(w_key), in_vmem(w_value)
    normed, kv = [], []
    for r in range(CHUNKS):
        n, y = project_kv(
            info, r, part, tokens, tm, x[r], xm[r], gain, wk, wv, cosine, sine
        )
        normed.append(n)
        kv.append(y)
    q = project_q(normed, w_query, cosine, sine)

    w_later, _ = lax.optimization_barrier((w_out, kv[-1]))
    wm = [
        across(lax.dynamic_slice_in_dim(w_later, (head ^ 1 ^ flip) * width, width, 1), 1)
        for flip in (0, 2)
    ]

    column, held = kv, []
    for k in range(n_ctx // 2):
        if k:
            column = [upward(v) for v in column]
        held.append(column + [neighbour(v) for v in column])

    last_step = n_ctx // 2 - 1
    runs = [(0, 2), (2, last_step), (last_step, last_step + 1)]
    state = None
    for lo, hi in runs:
        if lo >= hi:
            continue
        steps = [(k, b) for k in range(lo, hi) for b in range(2)]
        pieces = [v for k in range(lo, hi) for v in held[k]]
        state = attend(steps, pieces, info, q, starts, state, hi > last_step, kvh)
    (a,) = state
    am = across(a, 1)
    received = [
        across(project_out(info, 2, i, 1, a, am, w_out, wm, BF16), 2)
        for i in range(OUT_CHUNKS)
    ]
    mine = project_out(info, 0, 0, OUT_CHUNKS, a, am, w_out, wm, F32)
    early = OUT_CHUNKS - 1
    out = add_up(received[:early], 0, mine, tokens, None)
    return add_up(received[early:], early, mine, tokens, out)


def solution(mesh):
    in_specs = (
        P("ctx", "head"),
        P(),
        P(),
        P(None, "head"),
        P(None, "head"),
        P(None, "head"),
        P("head", None),
    )
    body = functools.partial(on_device, mesh.shape["ctx"], mesh.shape["head"])
    return jax.shard_map(
        body, mesh=mesh, in_specs=in_specs, out_specs=P("ctx", "head"), check_vma=False
    )
```
